128 devices in a mesh: dp: 4 (over z), row: 4 (over x_lo, core), col: 8 (over x_hi, y).
Axes of the slice: x: 4 (x_hi: 2, x_lo: 2; x = x_hi * 2 + x_lo), y: 4, z: 4, core: 2. Of those that a mesh axis runs over, the one named last changes fastest.
Arguments:
- activations: bfloat16 [4096, 18432], P(('dp', 'col'), 'row'), may hold values from -6 to 6
- cotangent: bfloat16 [4096, 16384], P(('dp', 'row'), 'col'), may hold values from -0.09375 to 0.09375
- weight: float32 [18432, 16384], P(('row', 'dp'), 'col'), may hold values from -60 to 60
- row_moment: float32 [18432], P(('row', 'dp')), may hold values from 0.05 to 1
- col_moment: float32 [16384], P('col'), may hold values from 0.05 to 1
Outputs:
- new_weight: float32 [18432, 16384], P(('row', 'dp'), 'col')
- clipped_update: bfloat16 [18432, 16384], P(('row', 'dp'), 'col')
- new_row_moment: float32 [18432], P(('row', 'dp'))
- new_col_moment: float32 [16384], P('col')
The draws below stay inside these ranges and needn't reach their ends.
All inputs are finite; a program needn't handle non-finite values.
Results may differ from the reference program's by a relative error of at most 0.001.
Values may be sent and summed in bfloat16 or wider, within the bound.
A program may use at most 192 MiB of HBM per device.

```python
import math
import jax
import jax.numpy as jnp
from jax import lax

D = 18432
F = 16384
STEP = 10
TOKENS = 4096


def draw_weight(key, part):
    key = jax.random.fold_in(key, 7)
    key_rows, key_cols, key_base = jax.random.split(key, 3)
    position = jnp.arange(D, dtype=jnp.float32) / D
    row_factor = 3.0 ** (position - 0.5) * 10.0 ** jax.random.uniform(key_rows, (D,), jnp.float32, -0.5, 0.5)
    col_factor = 10.0 ** jax.random.uniform(key_cols, (F,), jnp.float32, -0.25, 0.25)
    base_values = jnp.clip(jax.random.normal(key_base, (D, F), jnp.float32), -6.0, 6.0)
    return (base_values * row_factor[:, None] * col_factor[None, :]).astype(jnp.float32)


def spiked(result, stream_key, source, target, parts, factor):
    def block_of(dim):
        return (jnp.arange(result.shape[dim]) // (result.shape[dim] // parts)).reshape((-1,) + (1,) * (result.ndim - 1 - dim))

    first = jax.random.permutation(stream_key, parts)[block_of(target)]
    other_side = (block_of(target) + parts // 2) % parts
    return jnp.where((block_of(source) == first) | (block_of(source) == other_side), factor * result, result)


def levels(stream_key, shape, pieces, smallest, high):
    loudness = 1.0
    for dim, blocks in pieces:
        draws = jax.random.uniform(jax.random.fold_in(jax.random.fold_in(stream_key, 6), dim), (blocks,), jnp.float32, smallest / len(pieces), high / len(pieces))
        loudness = loudness * jnp.repeat(jnp.exp(draws), shape[dim] // blocks).reshape((-1,) + (1,) * (len(shape) - 1 - dim))
    return loudness


def noise(stream_key, dims, scale, limit, shards=(), held_as=jnp.bfloat16):
    gain = levels(stream_key, dims, shards, -0.22, 0.18) if shards else 1.0
    entries = jax.random.normal(stream_key, dims, jnp.float32) * scale * gain
    return jnp.minimum(jnp.maximum(entries, -limit), limit).astype(held_as)


def gaussian_with(own_key, extent, deviation, limit, cuts, heavy, kind=jnp.bfloat16):
    drawn = deviation * jax.random.normal(own_key, extent, jnp.float32)
    if cuts:
        drawn = drawn * levels(own_key, extent, cuts, -0.22, 0.18)
    return jnp.clip(spiked(drawn, jax.random.fold_in(own_key, 3), *heavy), -limit, limit).astype(kind)


def setup_inputs(seed: int = 0) -> dict:
    key_list = jax.random.split(jax.random.key(seed), 6)
    return {
        "activations": gaussian_with(key_list[0], (TOKENS, D), 1.0, 6.0, ((0, 32), (1, 4)), (0, 1, 32, 2.75)),
        "cotangent": noise(key_list[1], (TOKENS, F), TOKENS ** -0.5, 0.09375, ((0, 16), (1, 8))),
        "weight": draw_weight(jax.random.fold_in(key_list[5], 71), 0),
        "row_moment": jnp.clip(jnp.exp(math.log(1.0) - 2.9957323 * jax.random.uniform(key_list[3], (D,), jnp.float32) ** levels(key_list[3], (D,), ((0, 16),), -0.2, 0.2)), 0.05, 1.0),
        "col_moment": jnp.clip(jnp.exp(math.log(1.0) - 2.9957323 * jax.random.uniform(key_list[4], (F,), jnp.float32) ** levels(key_list[4], (F,), ((0, 8),), -0.2, 0.2)), 0.05, 1.0),
    }


def reference(activations, cotangent, weight, row_moment, col_moment):
    decay_rate = 1.0 - float(STEP) ** (-0.8)
    relative = min(0.01, float(STEP) ** (-0.5))
    gradient = jnp.dot(activations.T, cotangent, preferred_element_type=jnp.float32)
    squared = gradient * gradient
    row_new = decay_rate * row_moment + (1.0 - decay_rate) * lax.optimization_barrier(jnp.sum(squared, axis=1)) / F
    col_new = decay_rate * col_moment + (1.0 - decay_rate) * lax.optimization_barrier(jnp.sum(squared, axis=0)) / D
    update = gradient * lax.rsqrt(row_new)[:, None] * lax.rsqrt(col_new)[None, :]
    clip_factor = jnp.maximum(1.0, jnp.sqrt(jnp.sum(update * update) / (D * F)))
    clipped = update / clip_factor
    new_weight = weight - relative * clipped
    return (new_weight, clipped.astype(jnp.bfloat16), row_new, col_new)
```

```python
import functools

import jax
import jax.numpy as jnp
from jax import lax
from jax.experimental import pallas as pl
from jax.experimental.pallas import tpu as pltpu
from jax.sharding import PartitionSpec as P

D = 18432
F = 16384
STEP = 10
MESH = pl.DeviceIdType.MESH

ROWS = 1152
COLS = 2048
PIECE = 128
PIECES = 32
TILE = 512
SENDS = 62


def gather_kernel(
    act, cot, weight, row_m, col_m,
    u_ref, w_ref, scale_ref, row_out, col_out,
    a_in, a_src, at, ct, row_part, row_col, col_scale, row_x, col_x, tot_a, tot_b,
    load_sem, send_sem, a_sem, c_sem, own_sem, x_send, y_send, row_sem, col_sem, ta_sem, tb_sem,
):
    z, row, col = lax.axis_index("dp"), lax.axis_index("row"), lax.axis_index("col")
    x_lo, core = row // 2, row % 2
    x_hi, y = col // 4, col % 4
    group = z * 4 + row

    def a_id(zo, xo, yo):
        return ((z + zo + 4) % 4) * 8 + ((x_hi + xo) % 2) * 4 + (y + yo + 4) % 4

    def c_id(zo, xo, co, half):
        return ((z + zo + 4) % 4) * 8 + ((x_lo + xo) % 2) * 4 + ((core + co) % 2) * 2 + half

    def at_z(o):
        return {"dp": (z + o + 4) % 4, "row": row, "col": col}

    def at_y(o):
        return {"dp": z, "row": row, "col": x_hi * 4 + (y + o + 4) % 4}

    def at_x_hi():
        return {"dp": z, "row": row, "col": (1 - x_hi) * 4 + y}

    def at_x_lo():
        return {"dp": z, "row": (1 - x_lo) * 2 + core, "col": col}

    def at_core():
        return {"dp": z, "row": x_lo * 2 + 1 - core, "col": col}

    def col_peer(i):
        return {"dp": z, "row": row, "col": (col + i) % 8}

    def group_peer(i):
        g = (group + i) % 16
        return {"dp": g // 4, "row": g % 4, "col": col}

    barrier = pltpu.get_barrier_semaphore()

    def greet_col(i, carry):
        pl.semaphore_signal(barrier, inc=1, device_id=col_peer(i), device_id_type=MESH)
        return carry

    def greet_group(i, carry):
        pl.semaphore_signal(barrier, inc=1, device_id=group_peer(i), device_id_type=MESH)
        return carry

    load_act = pltpu.make_async_copy(act, a_in, load_sem.at[0])
    load_act.start()
    load_cot = []
    for half in range(2):
        load_cot.append(pltpu.make_async_copy(
            cot.at[pl.ds(half * PIECE, PIECE)], ct.at[c_id(0, 0, 0, half)], load_sem.at[1 + half]
        ))
        load_cot[half].start()
    lax.fori_loop(1, 8, greet_col, 0)
    lax.fori_loop(1, 16, greet_group, 0)

    sent = []

    def push(src, dst, sem, device):
        copy = pltpu.make_async_remote_copy(
            src_ref=src, dst_ref=dst, send_sem=send_sem.at[len(sent)], recv_sem=sem,
            device_id=device, device_id_type=MESH,
        )
        copy.start()
        sent.append(copy)

    def push_a(t, device):
        push(at.at[t], at.at[t], a_sem.at[t], device)

    def push_c(t, device):
        push(ct.at[t], ct.at[t], c_sem.at[t], device)

    def wait_a(zo, xo, yo):
        t = a_id(zo, xo, yo)
        pltpu.make_async_copy(at.at[t], at.at[t], a_sem.at[t]).wait()
        return t

    def wait_c(zo, xo, co, half):
        t = c_id(zo, xo, co, half)
        pltpu.make_async_copy(ct.at[t], ct.at[t], c_sem.at[t]).wait()
        return t

    def turned(slot, block):
        start = pl.multiple_of(slot * ROWS + block * 128, 128)
        return a_in[:, pl.ds(start, 128)].T

    def ring(t, *steps):
        for o in steps:
            push_a(t, at_y(o))

    load_act.wait()
    own = a_id(0, 0, 0)
    for block in range(ROWS // 128):
        at[own, pl.ds(block * 128, 128), :] = turned(z, block)
    pl.semaphore_wait(barrier, 22)
    ring(own, 1, -1)
    push_a(own, at_x_hi())
    for i, o in enumerate((1, -1, 2)):
        for block in range(ROWS // 128):
            a_src[i, pl.ds(block * 128, 128), :] = turned((z + o + 4) % 4, block)
        push(a_src.at[i], at.at[own], a_sem.at[own], at_z(o))
    for half in range(2):
        load_cot[half].wait()
    mine = [c_id(0, 0, 0, half) for half in range(2)]
    for half in range(2):
        push_c(mine[half], at_z(1))
        push_c(mine[1 - half], at_z(-1))
        push_c(mine[half], at_core())
    load_weight = pltpu.make_async_copy(weight, w_ref, load_sem.at[3])
    load_weight.start()

    def matmul(ids, first=False, last=False):
        def tile(j, carry):
            s = pl.ds(pl.multiple_of(j * TILE, TILE), TILE)
            left = jnp.concatenate([at[t] for t in ids], axis=1)
            right = jnp.concatenate([ct[t, :, s] for t in ids], axis=0)
            product = jnp.dot(left, right, preferred_element_type=jnp.float32)
            if not first:
                product = u_ref[:, s] + product
            u_ref[:, s] = product
            if last:
                square = product * product
                col_x[group, :, s] = jnp.sum(square, axis=0, keepdims=True)
                part = square[:, :128]
                for k in range(1, TILE // 128):
                    part = part + square[:, k * 128:(k + 1) * 128]
                row_part[...] += part
            return carry

        lax.fori_loop(0, COLS // TILE, tile, 0)

    def cot_group(zo, xo):
        return [c_id(zo, xo, co, half) for co in range(2) for half in range(2)]

    t = wait_a(0, 1, 0)
    ring(t, 1, -1)
    t = wait_a(1, 0, 0)
    ring(t, 1, -1)
    push_a(t, at_x_hi())
    t = wait_a(-1, 0, 0)
    push_a(t, at_x_hi())
    t = wait_a(2, 0, 0)
    push_a(t, at_x_hi())
    for half in range(2):
        push_c(mine[half], at_x_lo())
    ring(wait_a(0, 0, -1), 1)
    wait_a(0, 0, 1)
    ring(wait_a(0, 1, 1), -1)
    wait_a(0, 1, -1)
    ring(wait_a(1, 1, 0), 1, -1)
    ring(wait_a(1, 0, -1), 1)
    wait_a(1, 0, 1)
    ring(a_id(-1, 0, 0), 1, -1)
    third = wait_a(-1, 1, 0)
    ring(third, 1)
    for half in range(2):
        t = wait_c(-1, 0, 0, 0) if half == 0 else wait_c(1, 0, 0, 1)
        push_c(t, at_z(1 - 2 * half))
        push_c(t, at_core())
    wait_a(0, 0, 2)
    wait_a(0, 1, 2)
    for half in range(2):
        wait_c(0, 0, 1, half)
    row_x[col] = jnp.zeros((16, 128), jnp.float32)
    row_part[...] = jnp.zeros_like(row_part)
    matmul(cot_group(0, 0), first=True)
    ring(wait_a(1, 1, 1), -1)
    ring(third, -1)
    wait_a(1, 1, -1)
    push_c(wait_c(-1, 0, 0, 1), at_core())
    push_c(wait_c(1, 0, 0, 0), at_core())
    t = wait_c(0, 1, 0, 0)
    for device in (at_z(1), at_z(-1), at_core()):
        push_c(t, device)
    wait_a(-1, 0, 1)
    ring(wait_a(-1, 0, -1), 1)
    ring(a_id(2, 0, 0), 1)
    last = wait_a(2, 1, 0)
    ring(last, 1, -1)
    wait_a(1, 0, 2)
    wait_a(1, 1, 2)
    for zo in (1, -1):
        for half in range(2):
            wait_c(zo, 0, 1, half)
    matmul(cot_group(1, 0))
    for half in range(2):
        t = wait_c(2, 0, 0, half)
        push_c(t, at_x_lo())
        push_c(t, at_core())
    t = wait_c(0, 1, 0, 1)
    for device in (at_z(1), at_z(-1), at_core()):
        push_c(t, device)
    ring(wait_a(-1, 1, 1), -1)
    ring(a_id(2, 0, 0), -1)
    wait_a(-1, 1, -1)
    for half in range(2):
        wait_c(0, 1, 1, half)
    matmul(cot_group(0, 1))
    ring(wait_a(2, 1, 1), -1)
    for zo in (-1, 1):
        push_c(wait_c(zo, 1, 0, 0), at_core())
    ring(wait_a(2, 0, -1), 1)
    wait_a(-1, 0, 2)
    wait_a(-1, 1, 2)
    matmul(cot_group(-1, 0))
    push_c(wait_c(2, 1, 0, 0), at_core())
    for zo in (-1, 1):
        wait_c(zo, 1, 1, 0)
    matmul([c_id(zo, 1, co, 0) for zo in (-1, 1) for co in range(2)])
    for zo in (-1, 1):
        push_c(wait_c(zo, 1, 0, 1), at_core())
    push_c(wait_c(2, 1, 0, 1), at_core())
    for zo in (-1, 1):
        wait_c(zo, 1, 1, 1)
    matmul([c_id(zo, 1, co, 1) for zo in (-1, 1) for co in range(2)])
    for xo in range(2):
        for half in range(2):
            wait_c(2, xo, 1, half)
    wait_a(2, 0, 1)
    wait_a(2, 1, -1)
    matmul([a_id(2, xo, yo) for xo in range(2) for yo in (0, 1)])
    matmul([a_id(2, xo, -1) for xo in range(2)])
    wait_a(2, 0, 2)
    wait_a(2, 1, 2)
    matmul([a_id(2, xo, 2) for xo in range(2)], last=True)

    def small(buf, slot, sem, sends, peer, count):
        def descriptor(i):
            return pltpu.make_async_remote_copy(
                src_ref=buf.at[slot], dst_ref=buf.at[slot], send_sem=sends.at[i], recv_sem=sem.at[slot],
                device_id=peer(i), device_id_type=MESH,
            )

        def start(i, carry):
            descriptor(i).start()
            return carry

        def finish(i, carry):
            other = (slot + i) % count
            pltpu.make_async_copy(buf.at[other], buf.at[other], sem.at[other]).wait()
            return carry

        def drain(i, carry):
            descriptor(i).wait_send()
            return carry

        return (
            lambda: lax.fori_loop(1, count, start, 0),
            lambda: lax.fori_loop(1, count, finish, 0),
            lambda: lax.fori_loop(1, count, drain, 0),
        )

    col_start, col_finish, col_drain = small(col_x, group, col_sem, x_send, group_peer, 16)
    row_start, row_finish, row_drain = small(row_x, col, row_sem, y_send, col_peer, 8)
    col_start()
    for block in range(ROWS // 128):
        turned_part = row_part[pl.ds(block * 128, 128), :].T
        row_x[col, pl.ds(block, 1), :] = jnp.sum(turned_part, axis=0, keepdims=True)
    row_start()
    for copy in sent:
        copy.wait_send()
    load_weight.wait()

    decay_rate = 1.0 - float(STEP) ** (-0.8)
    col_finish()
    col_sum = col_x[0]
    for i in range(1, 16):
        col_sum = col_sum + col_x[i]
    col_new = decay_rate * col_m[...] + (1.0 - decay_rate) * col_sum / D
    col_out[...] = col_new
    col_scale[...] = lax.rsqrt(col_new)
    row_finish()
    row_sum = row_x[0]
    for i in range(1, 8):
        row_sum = row_sum + row_x[i]
    row_new = decay_rate * row_m[...] + (1.0 - decay_rate) * row_sum[: ROWS // 128] / F
    row_out[...] = row_new
    row_scale = lax.rsqrt(row_new)
    for block in range(ROWS // 128):
        spread = jnp.broadcast_to(row_scale[block:block + 1, :], (128, 128))
        row_col[pl.ds(block * 128, 128), :] = spread.T

    def scale_rows(block, total):
        r = pl.ds(pl.multiple_of(block * 64, 64), 64)
        factor = row_col[r, :]
        for k in range(COLS // 128):
            s = pl.ds(k * 128, 128)
            update = u_ref[r, s] * factor * col_scale[:, s]
            u_ref[r, s] = update
            total = total + update * update
        return total

    total = lax.fori_loop(0, ROWS // 64, scale_rows, jnp.zeros((64, 128), jnp.float32))
    tot_a[group] = jnp.sum(total.reshape(8, 8, 128), axis=0)
    col_drain()
    row_drain()
    a_start, a_finish, a_drain = small(tot_a, group, ta_sem, x_send, group_peer, 16)
    a_start()
    a_finish()
    total = tot_a[0]
    for i in range(1, 16):
        total = total + tot_a[i]
    tot_b[col] = total
    b_start, b_finish, b_drain = small(tot_b, col, tb_sem, y_send, col_peer, 8)
    b_start()
    a_drain()
    b_finish()
    total = tot_b[0]
    for i in range(1, 8):
        total = total + tot_b[i]
    mean = jnp.sum(total, keepdims=True) / (D * F)
    clip_factor = jnp.maximum(1.0, jnp.sqrt(mean))
    scale_ref[...] = jnp.broadcast_to(1.0 / clip_factor, (8, 128))
    b_drain()


def write_kernel(u_ref, w_ref, scale_ref, new_weight, clipped, stage_w, stage_c, sem):
    relative = min(0.01, float(STEP) ** (-0.5))
    height, slots = 128, 3
    steps = ROWS // height

    def copies(i):
        r = pl.ds(i * height, height)
        s = i % slots
        return (
            pltpu.make_async_copy(stage_w.at[s], new_weight.at[r], sem.at[s, 0]),
            pltpu.make_async_copy(stage_c.at[s], clipped.at[r], sem.at[s, 1]),
        )

    scale = scale_ref[0:1, :]
    for i in range(steps):
        if i >= slots:
            for copy in copies(i - slots):
                copy.wait()
        r = pl.ds(i * height, height)
        for k in range(COLS // 128):
            s = pl.ds(k * 128, 128)
            value = u_ref[r, s] * scale
            stage_c[i % slots, :, s] = value.astype(jnp.bfloat16)
            stage_w[i % slots, :, s] = w_ref[r, s] - relative * value
        for copy in copies(i):
            copy.start()
    for i in range(steps - slots, steps):
        for copy in copies(i):
            copy.wait()


def body(activations, cotangent, weight, row_moment, col_moment):
    f32, bf16 = jnp.float32, jnp.bfloat16
    vmem, anywhere = pl.BlockSpec(memory_space=pltpu.VMEM), pl.BlockSpec(memory_space=pl.ANY)
    update, held, scale, row_new, col_new = pl.pallas_call(
        gather_kernel,
        out_shape=(
            pltpu.VMEM((ROWS, COLS), f32),
            pltpu.VMEM((ROWS, COLS), f32),
            jax.ShapeDtypeStruct((8, 128), f32),
            jax.ShapeDtypeStruct((ROWS // 128, 128), f32),
            jax.ShapeDtypeStruct((1, COLS), f32),
        ),
        in_specs=[anywhere, anywhere, anywhere, vmem, vmem],
        out_specs=(vmem,) * 5,
        scratch_shapes=[
            pltpu.VMEM((PIECE, 4 * ROWS), bf16),
            pltpu.VMEM((3, ROWS, PIECE), bf16),
            pltpu.VMEM((PIECES, ROWS, PIECE), bf16),
            pltpu.VMEM((PIECES, PIECE, COLS), bf16),
            pltpu.VMEM((ROWS, 128), f32),
            pltpu.VMEM((ROWS, 128), f32),
            pltpu.VMEM((1, COLS), f32),
            pltpu.VMEM((8, 16, 128), f32),
            pltpu.VMEM((16, 1, COLS), f32),
            pltpu.VMEM((16, 8, 128), f32),
            pltpu.VMEM((8, 8, 128), f32),
            pltpu.SemaphoreType.DMA((4,)),
            pltpu.SemaphoreType.DMA((SENDS,)),
            pltpu.SemaphoreType.DMA((PIECES,)),
            pltpu.SemaphoreType.DMA((PIECES,)),
            pltpu.SemaphoreType.DMA((1,)),
            pltpu.SemaphoreType.DMA((16,)),
            pltpu.SemaphoreType.DMA((8,)),
            pltpu.SemaphoreType.DMA((8,)),
            pltpu.SemaphoreType.DMA((16,)),
            pltpu.SemaphoreType.DMA((16,)),
            pltpu.SemaphoreType.DMA((8,)),
        ],
        compiler_params=pltpu.CompilerParams(
            collective_id=0, has_side_effects=True, vmem_limit_bytes=36 << 20
        ),
    )(activations, cotangent, weight, row_moment.reshape(ROWS // 128, 128), col_moment.reshape(1, COLS))
    new_weight, clipped = pl.pallas_call(
        write_kernel,
        out_shape=(
            jax.ShapeDtypeStruct((ROWS, COLS), f32),
            jax.ShapeDtypeStruct((ROWS, COLS), bf16),
        ),
        in_specs=[vmem, vmem, vmem],
        out_specs=(anywhere, anywhere),
        scratch_shapes=[
            pltpu.VMEM((3, 128, COLS), f32),
            pltpu.VMEM((3, 128, COLS), bf16),
            pltpu.SemaphoreType.DMA((3, 2)),
        ],
        compiler_params=pltpu.CompilerParams(vmem_limit_bytes=16 << 20),
    )(update, held, scale)
    return new_weight, clipped, row_new.reshape(ROWS), col_new.reshape(COLS)


def solution(mesh):
    placed = (
        P(("dp", "col"), "row"),
        P(("dp", "row"), "col"),
        P(("row", "dp"), "col"),
        P(("row", "dp")),
        P("col"),
    )
    return jax.shard_map(
        body,
        mesh=mesh,
        in_specs=placed,
        out_specs=(P(("row", "dp"), "col"), P(("row", "dp"), "col"), P(("row", "dp")), P("col")),
        check_vma=False,
    )
```

```python
import functools

import jax
import jax.numpy as jnp
from jax import lax
from jax.experimental import pallas as pl
from jax.experimental.pallas import tpu as pltpu
from jax.sharding import PartitionSpec as P

D = 18432
F = 16384
STEP = 10
MESH = pl.DeviceIdType.MESH

ROWS = 1152
COLS = 2048
PIECE = 128
PIECES = 32
SENDS = 66


PARTS = {
    "a0": (0, ROWS // 2), "a1": (ROWS // 2, ROWS // 2),
    "c0": (0, 32), "c1": (32, 32), "c2": (64, 64),
}
PART_SEM = {"a0": 0, "a1": 1, "c0": 0, "c1": 1, "c2": 2}
ORDER = (
    ("c>", (0, 0, 0, 0), "z+"), ("a>", (0, 0, 0), "z-"), ("c>", (0, 0, 0, 0), "core"), ("c>", (0, 0, 0, 1), "core"),
    ("c>", (0, 0, 0, 1), "z-"), ("c>", (0, 0, 0, 0), "x"), ("c<", (0, 0, 1, 0)), ("c<", (0, 0, 1, 1)),
    ("a>", (0, 0, 0), "z+"), ("a<", (0, 0, -1)), ("a>", (0, 0, -1), "y+"), ("a<", (0, 0, 1)), ("a<", (1, 0, 0)),
    ("a>", (1, 0, 0), "y-"), ("a<", (0, 1, 0)), ("a>", (0, 1, 0), "y+"), ("a>", (0, 1, 0), "y-"),
    ("c<", (-1, 0, 0, 0)), ("c>", (-1, 0, 0, 0), "core"), ("c>", (-1, 0, 0, 0), "z+"), ("c>", (0, 0, 0, 0), "z-"),
    ("a>", (1, 0, 0), "xh"), ("c<", (-1, 0, 1, 0)), ("a<", (0, 0, 2)), ("a>", (1, 0, 0), "y+"), ("a<", (1, 0, 1)),
    ("a>", (1, 0, 1), "y-"), ("a<", (-1, 0, 0)), ("c<", (1, 0, 0, 1)), ("c>", (1, 0, 0, 1), "core"),
    ("a>", (-1, 0, 0), "xh"), ("c<", (0, 1, 0, 0)), ("c>", (0, 1, 0, 0), "core"), ("c<", (1, 0, 1, 1)),
    ("a<", (0, 1, -1)), ("a>", (-1, 0, 0), "y+"), ("a<", (0, 1, 1)), ("a>", (0, 1, 1), "y-"), ("c<", (0, 1, 1, 0)),
    ("a>", (0, 0, 0), "z2"), ("a<", (1, 1, 0)), ("c>", (0, 0, 0, 1), "x"), ("a<", (1, 0, -1)),
    ("a>", (1, 1, 0), "y+"), ("a<", (1, 0, 2)), ("a>", (1, 1, 0), "y-"), ("c<", (2, 0, 0, 0)),
    ("c>", (2, 0, 0, 0), "core"), ("c>", (0, 0, 0, 1), "z+"), ("c>", (1, 0, 0, 1), "z-"), ("c<", (1, 0, 0, 0)),
    ("c>", (1, 0, 0, 0), "core"), ("a<", (-1, 1, 0)), ("c<", (2, 0, 1, 0)), ("c<", (1, 0, 1, 0)), ("a<", (-1, 0, -1)),
    ("a>", (-1, 1, 0), "y+"), ("a<", (0, 1, 2)), ("a>", (-1, 0, 0), "y-"), ("mm", "zero_near"),
    ("c2>", (2, 0, 0, 0), "x"), ("a<", (2, 0, 0)), ("a<", (1, 1, -1)), ("a>", (2, 0, 0), "y+"), ("a<", (1, 1, 1)),
    ("a>", (2, 0, 0), "y-"), ("c>", (0, 1, 0, 0), "z+"), ("c>", (0, 1, 0, 0), "z-"), ("a>", (2, 0, 0), "xh"),
    ("c<", (0, 1, 0, 1)), ("c>", (0, 1, 0, 1), "core"), ("c<", (0, 1, 1, 1)), ("mm", "zero_far"),
    ("a0>", (-1, 0, -1), "y+"), ("a>", (-1, 1, 0), "y-"), ("a<", (-1, 1, -1)), ("a<", (-1, 0, 1)),
    ("c<", (-1, 0, 0, 1)), ("c>", (-1, 0, 0, 1), "core"), ("c<", (2, 0, 0, 1)), ("c>", (2, 0, 0, 1), "core"),
    ("a>", (1, 0, 2), "xh"), ("c2<", (2, 1, 0, 0)), ("a>", (-1, 1, -1), "y+"), ("c<", (-1, 0, 1, 1)),
    ("c<", (2, 0, 1, 1)), ("c>", (0, 1, 0, 1), "z+"), ("c>", (0, 1, 0, 1), "z-"), ("a<", (2, 0, -1)),
    ("a<", (2, 0, 1)), ("a1>", (-1, 0, 1), "y-"), ("a<", (2, 1, 0)), ("c>", (2, 0, 0, 1), "x"), ("a0<", (-1, 0, 2)),
    ("a>", (2, 1, 0), "y+"), ("a>", (2, 1, 0), "y-"), ("c<", (-1, 1, 0, 0)), ("c>", (-1, 1, 0, 0), "core"),
    ("c<", (1, 1, 0, 0)), ("c>", (1, 1, 0, 0), "core"), ("a<", (-1, 1, 1)), ("a<", (1, 1, 2)), ("mm", "plus_near"),
    ("a>", (2, 0, -1), "y+"), ("c0>", (-1, 1, 0, 0), "z+"), ("c1>", (1, 1, 0, 0), "z-"), ("c<", (-1, 1, 1, 0)),
    ("c<", (1, 1, 1, 0)), ("a<", (-1, 1, 2)), ("a1<", (-1, 0, 2)), ("mm", "minus_near"), ("mm", "far_0"),
    ("a<", (2, 1, -1)), ("a<", (2, 1, 1)), ("a>", (2, 1, 1), "y-"), ("c<", (-1, 1, 0, 1)),
    ("c>", (-1, 1, 0, 1), "core"), ("c<", (1, 1, 0, 1)), ("c>", (1, 1, 0, 1), "core"), ("mm", "two_near"),
    ("c<", (2, 1, 0, 1)), ("c>", (2, 1, 0, 1), "core"), ("c<", (-1, 1, 1, 1)), ("c0<", (2, 1, 0, 0)),
    ("c1<", (2, 1, 0, 0)), ("c>", (2, 1, 0, 0), "core"), ("c<", (1, 1, 1, 1)), ("mm", "far_1"), ("c<", (2, 1, 1, 1)),
    ("a<", (2, 0, 2)), ("c<", (2, 1, 1, 0)), ("mm", "two_far"), ("a<", (2, 1, 2)), ("mm", "two_last"),
)


def gather_kernel(
    act, cot, weight, row_m, col_m,
    g_ref, w_ref, row_col, col_scale, row_out, col_out,
    a_in, a_src, at, ct, row_part, row_x, col_x, tot_a, tot_b,
    load_sem, send_sem, a_sem, c_sem, x_send, y_send, ta_send, tb_send, row_sem, col_sem, ta_sem, tb_sem,
):
    z, row, col = lax.axis_index("dp"), lax.axis_index("row"), lax.axis_index("col")
    x_lo, core = row // 2, row % 2
    x_hi, y = col // 4, col % 4
    group = z * 4 + row
    z_at = {o: lax.rem(z + o + 4, 4) for o in (0, 1, -1, 2)}
    y_at = {o: lax.rem(y + o + 4, 4) for o in (0, 1, -1, 2)}
    x_hi_at, x_lo_at, core_at = (x_hi, 1 - x_hi), (x_lo, 1 - x_lo), (core, 1 - core)

    def a_id(zo, xo, yo):
        return z_at[zo] * 8 + x_hi_at[xo] * 4 + y_at[yo]

    def c_id(zo, xo, co, half):
        return z_at[zo] * 8 + x_lo_at[xo] * 4 + core_at[co] * 2 + half

    place = {
        "z+": {"dp": z_at[1], "row": row, "col": col},
        "z-": {"dp": z_at[-1], "row": row, "col": col},
        "z2": {"dp": z_at[2], "row": row, "col": col},
        "y+": {"dp": z, "row": row, "col": x_hi * 4 + y_at[1]},
        "y-": {"dp": z, "row": row, "col": x_hi * 4 + y_at[-1]},
        "xh": {"dp": z, "row": row, "col": (1 - x_hi) * 4 + y},
        "x": {"dp": z, "row": (1 - x_lo) * 2 + core, "col": col},
        "core": {"dp": z, "row": x_lo * 2 + 1 - core, "col": col},
    }

    def col_peer(i):
        return {"dp": z, "row": row, "col": lax.rem(col + i, 8)}

    def group_peer(i):
        return {"dp": lax.rem(z + i // 4, 4), "row": lax.rem(row + i, 4), "col": col}

    def group_slot(i):
        return lax.rem(z + i // 4, 4) * 4 + lax.rem(row + i, 4)

    def col_slot(i):
        return lax.rem(col + i, 8)

    offsets = (0, 1, -1, 2)
    load_act = []
    for i, o in enumerate(offsets):
        start = pl.multiple_of(z_at[o] * ROWS, 128)
        load_act.append(pltpu.make_async_copy(act.at[:, pl.ds(start, ROWS)], a_in.at[i], load_sem.at[i]))
        load_act[i].start()
    mine = [c_id(0, 0, 0, half) for half in range(2)]
    load_cot = []
    for half in range(2):
        load_cot.append(pltpu.make_async_copy(
            cot.at[pl.ds(half * PIECE, PIECE)], ct.at[mine[half]], load_sem.at[4 + half]
        ))
        load_cot[half].start()

    barrier = pltpu.get_barrier_semaphore()
    for where in place.values():
        pl.semaphore_signal(barrier, inc=1, device_id=where, device_id_type=MESH)

    sent = []

    def push(src, dst, sem, device):
        copy = pltpu.make_async_remote_copy(
            src_ref=src, dst_ref=dst, send_sem=send_sem.at[len(sent)], recv_sem=sem,
            device_id=device, device_id_type=MESH,
        )
        copy.start()
        sent.append(copy)

    def piece(kind, key):
        if kind[0] == "a":
            t, whole, sem = a_id(*key), at, a_sem
        else:
            t, whole, sem = c_id(*key), ct, c_sem
        if kind in PARTS:
            return whole.at[t, pl.ds(*PARTS[kind])], sem.at[PIECES + PART_SEM[kind]]
        return whole.at[t], sem.at[t]

    def send(kind, key, where):
        ref, sem = piece(kind, key)
        push(ref, ref, sem, place[where])

    own = a_id(0, 0, 0)

    def turn(i, out):
        load_act[i].wait()
        for block in range(ROWS // 128):
            r = pl.ds(block * 128, 128)
            out[r, :] = a_in[i, :, r].T

    turn(0, at.at[own])
    pl.semaphore_wait(barrier, 8)
    for where in ("y+", "y-", "xh"):
        send("a", (0, 0, 0), where)
    for half in range(2):
        load_cot[half].wait()
    load_weight = pltpu.make_async_copy(weight, w_ref, load_sem.at[6])

    def matmul(ids, first=False, last=False, width=1024):
        def tile(j, carry):
            s = pl.ds(pl.multiple_of(j * width, width), width)
            left = jnp.concatenate([at[t] for t in ids], axis=1)
            right = jnp.concatenate([ct[t, :, s] for t in ids], axis=0)
            product = jnp.dot(left, right, preferred_element_type=jnp.float32)
            if not first:
                product = g_ref[:, s] + product
            g_ref[:, s] = product
            if last:
                square = product * product
                col_x[group, :, s] = jnp.sum(square, axis=0, keepdims=True)
                part = square[:, :128]
                for k in range(1, width // 128):
                    part = part + square[:, k * 128:(k + 1) * 128]
                row_part[...] += part
            return carry

        lax.fori_loop(0, COLS // width, tile, 0)

    def cot_group(zo, xo):
        return [c_id(zo, xo, co, half) for co in range(2) for half in range(2)]

    def far(half):
        return [c_id(zo, 1, co, half) for zo in (-1, 1) for co in range(2)]

    def early(half):
        return [z_at[2] * 8 + half * 4 + y_at[yo] for yo in (0, 1, -1)]

    groups = {
        "zero_near": cot_group(0, 0),
        "zero_far": cot_group(0, 1),
        "plus_near": cot_group(1, 0),
        "minus_near": cot_group(-1, 0),
        "far_0": far(0),
        "far_1": far(1),
        "two_near": early(x_lo),
        "two_far": early(1 - x_lo),
        "two_last": [a_id(2, xo, 2) for xo in range(2)],
    }

    multiplied = 0
    for step in ORDER:
        if step[0] == "mm":
            if multiplied == 0:
                load_weight.start()
                row_part[...] = jnp.zeros_like(row_part)
                row_x[col] = jnp.zeros((16, 128), jnp.float32)
            multiplied += 1
            final = multiplied == len(groups)
            matmul(groups[step[1]], first=multiplied == 1, last=final, width=512 if final else 1024)
        elif step[0][-1] == ">":
            if step[0] == "a>" and step[1] == (0, 0, 0):
                i = ("z+", "z-", "z2").index(step[2])
                turn(i + 1, a_src.at[i])
                push(a_src.at[i], at.at[own], a_sem.at[own], place[step[2]])
            else:
                send(step[0][:-1], step[1], step[2])
        else:
            ref, sem = piece(step[0][:-1], step[1])
            pltpu.make_async_copy(ref, ref, sem).wait()

    def spread(buf, slot, sem, sends, peer, slots, count):
        copies = []
        for i in range(1, count):
            copies.append(pltpu.make_async_remote_copy(
                src_ref=buf.at[slot], dst_ref=buf.at[slot], send_sem=sends.at[i], recv_sem=sem.at[slot],
                device_id=peer(i), device_id_type=MESH,
            ))
            copies[-1].start()

        def collect():
            for i in range(1, count):
                other = slots(i)
                pltpu.make_async_copy(buf.at[other], buf.at[other], sem.at[other]).wait()
            total = buf[0]
            for i in range(1, count):
                total = total + buf[i]
            return total

        sent.extend(copies)
        return collect

    col_collect = spread(col_x, group, col_sem, x_send, group_peer, group_slot, 16)
    for block in range(ROWS // 128):
        turned_part = row_part[pl.ds(block * 128, 128), :].T
        row_x[col, pl.ds(block, 1), :] = jnp.sum(turned_part, axis=0, keepdims=True)
    row_collect = spread(row_x, col, row_sem, y_send, col_peer, col_slot, 8)

    decay_rate = 1.0 - float(STEP) ** (-0.8)
    col_new = decay_rate * col_m[...] + (1.0 - decay_rate) * col_collect() / D
    col_out[...] = col_new
    col_scale[...] = lax.rsqrt(col_new)
    row_new = decay_rate * row_m[...] + (1.0 - decay_rate) * row_collect()[: ROWS // 128] / F
    row_out[...] = row_new
    row_scale = lax.rsqrt(row_new)
    for block in range(ROWS // 128):
        across = jnp.broadcast_to(row_scale[block:block + 1, :], (128, 128))
        row_col[pl.ds(block * 128, 128), :] = across.T

    def square_rows(block, total):
        r = pl.ds(pl.multiple_of(block * 64, 64), 64)
        line = jnp.zeros((64, 128), jnp.float32)
        for k in range(COLS // 128):
            s = pl.ds(k * 128, 128)
            value = g_ref[r, s] * col_scale[:, s]
            line = line + value * value
        factor = row_col[r, :]
        return total + line * factor * factor

    total = lax.fori_loop(0, ROWS // 64, square_rows, jnp.zeros((64, 128), jnp.float32))
    tot_a[group] = jnp.sum(total.reshape(8, 8, 128), axis=0)
    a_collect = spread(tot_a, group, ta_sem, ta_send, group_peer, group_slot, 16)
    tot_b[col] = a_collect()
    b_collect = spread(tot_b, col, tb_sem, tb_send, col_peer, col_slot, 8)
    for copy in sent:
        copy.wait_send()
    load_weight.wait()
    mean = jnp.sum(b_collect(), keepdims=True) / (D * F)
    clip_factor = jnp.maximum(1.0, jnp.sqrt(mean))
    col_scale[...] = col_scale[...] / clip_factor


def write_kernel(
    g_ref, w_ref, row_col, col_scale, row_new, col_new,
    new_weight, clipped, row_out, col_out, stage_w, stage_c, sem,
):
    relative = min(0.01, float(STEP) ** (-0.5))
    height, slots = 64, 6
    steps = ROWS // height

    def copies(i):
        r = pl.ds(i * height, height)
        s = i % slots
        return (
            pltpu.make_async_copy(stage_w.at[s], new_weight.at[r], sem.at[s, 0]),
            pltpu.make_async_copy(stage_c.at[s], clipped.at[r], sem.at[s, 1]),
        )

    for i in range(steps):
        if i >= slots:
            for copy in copies(i - slots):
                copy.wait()
        r = pl.ds(i * height, height)
        factor = row_col[r, :]
        for k in range(COLS // 128):
            s = pl.ds(k * 128, 128)
            value = g_ref[r, s] * factor * col_scale[:, s]
            stage_c[i % slots, :, s] = value.astype(jnp.bfloat16)
            stage_w[i % slots, :, s] = w_ref[r, s] - relative * value
        for copy in copies(i):
            copy.start()
    for block in range(ROWS // 128):
        row_out[pl.ds(block * 128, 128)] = row_new[block, :]
    for block in range(COLS // 128):
        col_out[pl.ds(block * 128, 128)] = col_new[0, block * 128:(block + 1) * 128]
    for i in range(steps - slots, steps):
        for copy in copies(i):
            copy.wait()


def body(activations, cotangent, weight, row_moment, col_moment):
    f32, bf16 = jnp.float32, jnp.bfloat16
    vmem, anywhere = pl.BlockSpec(memory_space=pltpu.VMEM), pl.BlockSpec(memory_space=pl.ANY)
    held = pl.pallas_call(
        gather_kernel,
        out_shape=(
            pltpu.VMEM((ROWS, COLS), f32),
            pltpu.VMEM((ROWS, COLS), f32),
            pltpu.VMEM((ROWS, 128), f32),
            pltpu.VMEM((1, COLS), f32),
            pltpu.VMEM((ROWS // 128, 128), f32),
            pltpu.VMEM((1, COLS), f32),
        ),
        in_specs=[anywhere, anywhere, anywhere, vmem, vmem],
        out_specs=(vmem,) * 6,
        scratch_shapes=[
            pltpu.VMEM((4, PIECE, ROWS), bf16),
            pltpu.VMEM((3, ROWS, PIECE), bf16),
            pltpu.VMEM((PIECES, ROWS, PIECE), bf16),
            pltpu.VMEM((PIECES, PIECE, COLS), bf16),
            pltpu.VMEM((ROWS, 128), f32),
            pltpu.VMEM((8, 16, 128), f32),
            pltpu.VMEM((16, 1, COLS), f32),
            pltpu.VMEM((16, 8, 128), f32),
            pltpu.VMEM((8, 8, 128), f32),
            pltpu.SemaphoreType.DMA((7,)),
            pltpu.SemaphoreType.DMA((SENDS,)),
            pltpu.SemaphoreType.DMA((PIECES + 2,)),
            pltpu.SemaphoreType.DMA((PIECES + 3,)),
            pltpu.SemaphoreType.DMA((16,)),
            pltpu.SemaphoreType.DMA((8,)),
            pltpu.SemaphoreType.DMA((16,)),
            pltpu.SemaphoreType.DMA((8,)),
            pltpu.SemaphoreType.DMA((8,)),
            pltpu.SemaphoreType.DMA((16,)),
            pltpu.SemaphoreType.DMA((16,)),
            pltpu.SemaphoreType.DMA((8,)),
        ],
        compiler_params=pltpu.CompilerParams(
            collective_id=0, has_side_effects=True, vmem_limit_bytes=38 << 20
        ),
    )(activations, cotangent, weight, row_moment.reshape(ROWS // 128, 128), col_moment.reshape(1, COLS))
    return pl.pallas_call(
        write_kernel,
        out_shape=(
            jax.ShapeDtypeStruct((ROWS, COLS), f32),
            jax.ShapeDtypeStruct((ROWS, COLS), bf16),
            jax.ShapeDtypeStruct((ROWS,), f32),
            jax.ShapeDtypeStruct((COLS,), f32),
        ),
        in_specs=[vmem] * 6,
        out_specs=(anywhere, anywhere, vmem, vmem),
        scratch_shapes=[
            pltpu.VMEM((6, 64, COLS), f32),
            pltpu.VMEM((6, 64, COLS), bf16),
            pltpu.SemaphoreType.DMA((6, 2)),
        ],
        compiler_params=pltpu.CompilerParams(vmem_limit_bytes=16 << 20),
    )(*held)


def solution(mesh):
    placed = (
        P(("dp", "col"), "row"),
        P(("dp", "row"), "col"),
        P(("row", "dp"), "col"),
        P(("row", "dp")),
        P("col"),
    )
    return jax.shard_map(
        body,
        mesh=mesh,
        in_specs=placed,
        out_specs=(P(("row", "dp"), "col"), P(("row", "dp"), "col"), P(("row", "dp")), P("col")),
        check_vma=False,
    )
```

```python
import functools

import jax
import jax.numpy as jnp
from jax import lax
from jax.experimental import pallas as pl
from jax.experimental.pallas import tpu as pltpu
from jax.sharding import PartitionSpec as P

D = 18432
F = 16384
STEP = 10
MESH = pl.DeviceIdType.MESH

ROWS = 1152
COLS = 2048
PIECE = 128
PIECES = 32
SENDS = 66


PARTS = {
    "a0": (0, ROWS // 2), "a1": (ROWS // 2, ROWS // 2),
    "c0": (0, 32), "c1": (32, 32), "c2": (64, 64),
}
PART_SEM = {"a0": 0, "a1": 1, "c0": 0, "c1": 1, "c2": 2}
ORDER = (
    ("a>", (0, 0, 0), "z+"), ("a>", (0, 0, 0), "z-"), ("c>", (0, 0, 0, 0), "core"), ("c>", (0, 0, 0, 1), "core"),
    ("c>", (0, 0, 0, 0), "z+"), ("c>", (0, 0, 0, 1), "z-"), ("c>", (0, 0, 0, 1), "x"), ("c<", (0, 0, 1, 0)),
    ("c<", (0, 0, 1, 1)), ("a<", (0, 0, -1)), ("a0>", (0, 0, -1), "y+"), ("a<", (0, 0, 1)), ("a1>", (0, 0, 1), "y-"),
    ("a<", (-1, 0, 0)), ("a>", (-1, 0, 0), "y+"), ("a>", (-1, 0, 0), "y-"), ("a<", (1, 0, 0)), ("a<", (0, 1, 0)),
    ("a0<", (0, 0, 2)), ("a>", (0, 1, 0), "y+"), ("a1<", (0, 0, 2)), ("a>", (0, 1, 0), "y-"), ("a>", (0, 0, 0), "z2"),
    ("a>", (1, 0, 0), "xh"), ("a<", (-1, 0, -1)), ("a>", (1, 0, 0), "y+"), ("a<", (-1, 0, 1)),
    ("a>", (1, 0, 0), "y-"), ("c<", (-1, 0, 0, 0)), ("c>", (-1, 0, 0, 0), "core"), ("c>", (0, 0, 0, 1), "z+"),
    ("c>", (0, 0, 0, 0), "z-"), ("a>", (-1, 0, 0), "xh"), ("c<", (1, 0, 0, 1)), ("c>", (1, 0, 0, 1), "core"),
    ("c<", (0, 1, 0, 1)), ("c>", (0, 1, 0, 1), "core"), ("c<", (-1, 0, 1, 0)), ("c<", (1, 0, 1, 1)),
    ("c<", (0, 1, 1, 1)), ("a<", (0, 1, -1)), ("a>", (-1, 0, -1), "y+"), ("a<", (0, 1, 1)), ("a>", (0, 1, 1), "y-"),
    ("a<", (2, 0, 0)), ("a<", (1, 1, 0)), ("a>", (2, 0, 0), "xh"), ("c>", (-1, 0, 0, 0), "z+"),
    ("c>", (0, 1, 0, 1), "z-"), ("a<", (1, 0, -1)), ("a>", (1, 1, 0), "y+"), ("a<", (1, 0, 1)),
    ("a>", (1, 1, 0), "y-"), ("a<", (-1, 1, 0)), ("c>", (0, 0, 0, 0), "x"), ("c<", (-1, 0, 0, 1)),
    ("c>", (-1, 0, 0, 1), "core"), ("c<", (1, 0, 0, 0)), ("c>", (1, 0, 0, 0), "core"), ("a<", (-1, 0, 2)),
    ("a>", (-1, 1, 0), "y+"), ("a<", (0, 1, 2)), ("a>", (-1, 1, 0), "y-"), ("mm", "zero_near"), ("a<", (2, 1, 0)),
    ("c<", (-1, 0, 1, 1)), ("c<", (1, 0, 1, 0)), ("c>", (0, 1, 0, 1), "z+"), ("c>", (1, 0, 0, 1), "z-"),
    ("a>", (-1, 0, 2), "xh"), ("a<", (1, 1, -1)), ("a>", (1, 1, -1), "y+"), ("a<", (1, 1, 1)),
    ("a>", (1, 0, 1), "y-"), ("mm", "plus_near"), ("c<", (2, 0, 0, 0)), ("c>", (2, 0, 0, 0), "core"),
    ("c<", (1, 1, 0, 1)), ("c>", (1, 1, 0, 1), "core"), ("c<", (0, 1, 0, 0)), ("c>", (0, 1, 0, 0), "core"),
    ("c>", (2, 0, 0, 0), "x"), ("a<", (-1, 1, -1)), ("a>", (2, 0, 0), "y+"), ("c<", (2, 0, 1, 0)),
    ("a>", (2, 1, 0), "y-"), ("a<", (-1, 1, 1)), ("mm", "minus_near"), ("c<", (1, 1, 1, 1)), ("c<", (0, 1, 1, 0)),
    ("mm", "zero_far"), ("c>", (0, 1, 0, 0), "z+"), ("c>", (0, 1, 0, 0), "z-"), ("a<", (-1, 1, 2)), ("a<", (1, 1, 2)),
    ("a>", (2, 1, 0), "y+"), ("a<", (1, 0, 2)), ("a>", (2, 0, 0), "y-"), ("mm", "near_last"), ("c<", (-1, 1, 0, 1)),
    ("c>", (-1, 1, 0, 1), "core"), ("c<", (2, 0, 0, 1)), ("c>", (2, 0, 0, 1), "core"), ("mm", "far_1_0"),
    ("c2>", (2, 0, 0, 1), "x"), ("c<", (-1, 1, 1, 1)), ("mm", "far_1_1"), ("c<", (2, 0, 1, 1)), ("a<", (2, 0, -1)),
    ("a>", (2, 0, -1), "y+"), ("a<", (2, 1, 1)), ("a>", (2, 1, 1), "y-"), ("c0>", (-1, 1, 0, 1), "z+"),
    ("c1>", (1, 1, 0, 1), "z-"), ("c<", (2, 1, 0, 0)), ("c>", (2, 1, 0, 0), "core"), ("a<", (2, 1, -1)),
    ("a<", (2, 0, 1)), ("mm", "two_near"), ("c<", (2, 1, 1, 0)), ("c<", (-1, 1, 0, 0)), ("c>", (-1, 1, 0, 0), "core"),
    ("c<", (1, 1, 0, 0)), ("c>", (1, 1, 0, 0), "core"), ("mm", "far_0_0"), ("c2<", (2, 1, 0, 1)),
    ("c0<", (2, 1, 0, 1)), ("c1<", (2, 1, 0, 1)), ("c>", (2, 1, 0, 1), "core"), ("mm", "two_side"),
    ("c<", (-1, 1, 1, 0)), ("c<", (1, 1, 1, 0)), ("mm", "far_0_1"), ("a<", (2, 0, 2)), ("a<", (2, 1, 2)),
    ("c<", (2, 1, 1, 1)), ("mm", "two_last"),
)


def gather_kernel(
    act, cot, weight, row_m, col_m,
    g_ref, w_ref, row_col, col_scale, row_out, col_out,
    a_in, a_src, at, ct, row_part, row_x, col_x, tot_a, tot_b,
    load_sem, send_sem, a_sem, c_sem, x_send, y_send, ta_send, tb_send, row_sem, col_sem, ta_sem, tb_sem,
):
    z, row, col = lax.axis_index("dp"), lax.axis_index("row"), lax.axis_index("col")
    x_lo, core = row // 2, row % 2
    x_hi, y = col // 4, col % 4
    group = z * 4 + row
    z_at = {o: lax.rem(z + o + 4, 4) for o in (0, 1, -1, 2)}
    y_at = {o: lax.rem(y + o + 4, 4) for o in (0, 1, -1, 2)}
    x_hi_at, x_lo_at, core_at = (x_hi, 1 - x_hi), (x_lo, 1 - x_lo), (core, 1 - core)

    def a_id(zo, xo, yo):
        return z_at[zo] * 8 + x_hi_at[xo] * 4 + y_at[yo]

    half_at = (lax.rem(y + 1, 2), lax.rem(y, 2))

    def c_id(zo, xo, co, half):
        return z_at[zo] * 8 + x_lo_at[xo] * 4 + core_at[co] * 2 + half_at[half]

    place = {
        "z+": {"dp": z_at[1], "row": row, "col": col},
        "z-": {"dp": z_at[-1], "row": row, "col": col},
        "z2": {"dp": z_at[2], "row": row, "col": col},
        "y+": {"dp": z, "row": row, "col": x_hi * 4 + y_at[1]},
        "y-": {"dp": z, "row": row, "col": x_hi * 4 + y_at[-1]},
        "xh": {"dp": z, "row": row, "col": (1 - x_hi) * 4 + y},
        "x": {"dp": z, "row": (1 - x_lo) * 2 + core, "col": col},
        "core": {"dp": z, "row": x_lo * 2 + 1 - core, "col": col},
    }

    def col_peer(i):
        return {"dp": z, "row": row, "col": lax.rem(col + i, 8)}

    def group_peer(i):
        return {"dp": lax.rem(z + i // 4, 4), "row": lax.rem(row + i, 4), "col": col}

    def group_slot(i):
        return lax.rem(z + i // 4, 4) * 4 + lax.rem(row + i, 4)

    def col_slot(i):
        return lax.rem(col + i, 8)

    def plane_peer(i):
        return {
            "dp": lax.rem(z + i // 8, 4), "row": lax.rem(row + i // 2 % 4, 4), "col": lax.rem(x_hi + i % 2, 2) * 4 + y,
        }

    def plane_slot(i):
        return (lax.rem(z + i // 8, 4) * 4 + lax.rem(row + i // 2 % 4, 4)) * 2 + lax.rem(x_hi + i % 2, 2)

    def y_peer(i):
        return {"dp": z, "row": row, "col": x_hi * 4 + lax.rem(y + i, 4)}

    def y_slot(i):
        return lax.rem(y + i, 4)

    offsets = (0, 1, -1, 2)
    load_act = []
    for i, o in enumerate(offsets):
        start = pl.multiple_of(z_at[o] * ROWS, 128)
        load_act.append(pltpu.make_async_copy(act.at[:, pl.ds(start, ROWS)], a_in.at[i], load_sem.at[i]))
        load_act[i].start()
    mine_at = z * 8 + x_lo * 4 + core * 2
    load_cot = []
    for half in range(2):
        load_cot.append(pltpu.make_async_copy(
            cot.at[pl.ds(half * PIECE, PIECE)], ct.at[mine_at + half], load_sem.at[4 + half]
        ))
        load_cot[half].start()

    barrier = pltpu.get_barrier_semaphore()
    for where in place.values():
        pl.semaphore_signal(barrier, inc=1, device_id=where, device_id_type=MESH)

    sent = []

    def push(src, dst, sem, device):
        copy = pltpu.make_async_remote_copy(
            src_ref=src, dst_ref=dst, send_sem=send_sem.at[len(sent)], recv_sem=sem,
            device_id=device, device_id_type=MESH,
        )
        copy.start()
        sent.append(copy)

    def piece(kind, key):
        if kind[0] == "a":
            t, whole, sem = a_id(*key), at, a_sem
        else:
            t, whole, sem = c_id(*key), ct, c_sem
        if kind in PARTS:
            return whole.at[t, pl.ds(*PARTS[kind])], sem.at[PIECES + PART_SEM[kind]]
        return whole.at[t], sem.at[t]

    def send(kind, key, where):
        ref, sem = piece(kind, key)
        push(ref, ref, sem, place[where])

    own = a_id(0, 0, 0)

    def turn(i, out):
        load_act[i].wait()
        for block in range(ROWS // 128):
            r = pl.ds(block * 128, 128)
            out[r, :] = a_in[i, :, r].T

    turn(0, at.at[own])
    pl.semaphore_wait(barrier, 8)
    for where in ("y+", "y-", "xh"):
        send("a", (0, 0, 0), where)
    for half in range(2):
        load_cot[half].wait()
    load_weight = pltpu.make_async_copy(weight, w_ref, load_sem.at[6])

    def matmul(ids, first=False, last=False, width=1024):
        def tile(j, carry):
            s = pl.ds(pl.multiple_of(j * width, width), width)
            left = jnp.concatenate([at[t] for t in ids], axis=1)
            right = jnp.concatenate([ct[t, :, s] for t in ids], axis=0)
            product = jnp.dot(left, right, preferred_element_type=jnp.float32)
            if not first:
                product = g_ref[:, s] + product
            g_ref[:, s] = product
            if last:
                square = product * product
                col_x[group, :, s] = jnp.sum(square, axis=0, keepdims=True)
                part = square[:, :128]
                for k in range(1, width // 128):
                    part = part + square[:, k * 128:(k + 1) * 128]
                row_part[...] += part
            return carry

        lax.fori_loop(0, COLS // width, tile, 0)

    def cot_group(zo, xo):
        return [c_id(zo, xo, co, half) for co in range(2) for half in range(2)]

    def far(half, *planes):
        return [c_id(zo, 1, co, half) for zo in (-1, 1) for co in planes]

    def meet(zo, xo, *steps):
        return [z_at[zo] * 8 + x_lo_at[xo] * 4 + y_at[yo] for yo in steps]

    groups = {
        "zero_near": cot_group(0, 0),
        "zero_far": cot_group(0, 1),
        "plus_near": meet(1, 0, 0, 1, -1),
        "minus_near": meet(-1, 0, 0, 1, -1),
        "near_last": meet(1, 0, 2) + meet(-1, 0, 2),
        "far_0": far(0, 0, 1),
        "far_1": far(1, 0, 1),
        "far_0_0": far(0, 0),
        "far_0_1": far(0, 1),
        "far_1_0": far(1, 0),
        "far_1_1": far(1, 1),
        "two_near": meet(2, 0, 0, 1, -1),
        "two_side": meet(2, 1, 1, -1),
        "two_last": meet(2, 1, 0, 2) + meet(2, 0, 2),
    }
    rounds = len([step for step in ORDER if step[0] == "mm"])

    multiplied = 0
    for step in ORDER:
        if step[0] == "mm":
            if multiplied == 0:
                load_weight.start()
                row_part[...] = jnp.zeros_like(row_part)
            multiplied += 1
            final = multiplied == rounds
            matmul(groups[step[1]], first=multiplied == 1, last=final, width=512 if final else 1024)
        elif step[0][-1] == ">":
            if step[0] == "a>" and step[1] == (0, 0, 0):
                i = ("z+", "z-", "z2").index(step[2])
                turn(i + 1, a_src.at[i])
                push(a_src.at[i], at.at[own], a_sem.at[own], place[step[2]])
            else:
                send(step[0][:-1], step[1], step[2])
        else:
            ref, sem = piece(step[0][:-1], step[1])
            pltpu.make_async_copy(ref, ref, sem).wait()

    def spread(buf, slot, sem, sends, peer, slots, count):
        copies = []
        for i in range(1, count):
            copies.append(pltpu.make_async_remote_copy(
                src_ref=buf.at[slot], dst_ref=buf.at[slot], send_sem=sends.at[i], recv_sem=sem.at[slot],
                device_id=peer(i), device_id_type=MESH,
            ))
            copies[-1].start()

        def collect():
            for i in range(1, count):
                other = slots(i)
                pltpu.make_async_copy(buf.at[other], buf.at[other], sem.at[other]).wait()
            total = buf[0]
            for i in range(1, count):
                total = total + buf[i]
            return total

        sent.extend(copies)
        return collect

    col_collect = spread(col_x, group, col_sem, x_send, group_peer, group_slot, 16)
    for block in range(ROWS // 128):
        turned_part = row_part[pl.ds(block * 128, 128), :].T
        row_x[col, pl.ds(block, 1), :] = jnp.sum(turned_part, axis=0, keepdims=True)
    row_collect = spread(row_x, col, row_sem, y_send, col_peer, col_slot, 8)

    decay_rate = 1.0 - float(STEP) ** (-0.8)
    col_new = decay_rate * col_m[...] + (1.0 - decay_rate) * col_collect() / D
    col_out[...] = col_new
    col_scale[...] = lax.rsqrt(col_new)
    row_new = decay_rate * row_m[...] + (1.0 - decay_rate) * row_collect() / F
    row_out[...] = row_new
    row_scale = lax.rsqrt(row_new)
    for block in range(ROWS // 128):
        across = jnp.broadcast_to(row_scale[block:block + 1, :], (128, 128))
        row_col[pl.ds(block * 128, 128), :] = across.T

    def square_rows(block, total):
        r = pl.ds(pl.multiple_of(block * 64, 64), 64)
        line = jnp.zeros((64, 128), jnp.float32)
        for k in range(COLS // 128):
            s = pl.ds(k * 128, 128)
            value = g_ref[r, s] * col_scale[:, s]
            line = line + value * value
        factor = row_col[r, :]
        return total + line * factor * factor

    total = lax.fori_loop(0, ROWS // 64, square_rows, jnp.zeros((64, 128), jnp.float32))
    plane = group * 2 + x_hi
    tot_a[plane] = jnp.sum(total, axis=0, keepdims=True)
    a_collect = spread(tot_a, plane, ta_sem, ta_send, plane_peer, plane_slot, 32)
    tot_b[y] = a_collect()
    b_collect = spread(tot_b, y, tb_sem, tb_send, y_peer, y_slot, 4)
    for copy in sent:
        copy.wait_send()
    load_weight.wait()
    mean = jnp.sum(b_collect(), keepdims=True) / (D * F)
    clip_factor = jnp.maximum(1.0, jnp.sqrt(mean))
    col_scale[...] = col_scale[...] / clip_factor


def write_kernel(
    g_ref, w_ref, row_col, col_scale, row_new, col_new,
    new_weight, clipped, row_out, col_out, stage_w, stage_c, sem,
):
    relative = min(0.01, float(STEP) ** (-0.5))
    height, slots = 64, 6
    steps = ROWS // height

    def copies(i):
        r = pl.ds(i * height, height)
        s = i % slots
        return (
            pltpu.make_async_copy(stage_w.at[s], new_weight.at[r], sem.at[s, 0]),
            pltpu.make_async_copy(stage_c.at[s], clipped.at[r], sem.at[s, 1]),
        )

    for i in range(steps):
        if i >= slots:
            for copy in copies(i - slots):
                copy.wait()
        r = pl.ds(i * height, height)
        factor = row_col[r, :]
        for k in range(COLS // 128):
            s = pl.ds(k * 128, 128)
            value = g_ref[r, s] * factor * col_scale[:, s]
            stage_c[i % slots, :, s] = value.astype(jnp.bfloat16)
            stage_w[i % slots, :, s] = w_ref[r, s] - relative * value
        for copy in copies(i):
            copy.start()
    for block in range(ROWS // 128):
        row_out[pl.ds(block * 128, 128)] = row_new[block, :]
    for block in range(COLS // 128):
        col_out[pl.ds(block * 128, 128)] = col_new[0, block * 128:(block + 1) * 128]
    for i in range(steps - slots, steps):
        for copy in copies(i):
            copy.wait()


def body(activations, cotangent, weight, row_moment, col_moment):
    f32, bf16 = jnp.float32, jnp.bfloat16
    vmem, anywhere = pl.BlockSpec(memory_space=pltpu.VMEM), pl.BlockSpec(memory_space=pl.ANY)
    held = pl.pallas_call(
        gather_kernel,
        out_shape=(
            pltpu.VMEM((ROWS, COLS), f32),
            pltpu.VMEM((ROWS, COLS), f32),
            pltpu.VMEM((ROWS, 128), f32),
            pltpu.VMEM((1, COLS), f32),
            pltpu.VMEM((ROWS // 128, 128), f32),
            pltpu.VMEM((1, COLS), f32),
        ),
        in_specs=[anywhere, anywhere, anywhere, vmem, vmem],
        out_specs=(vmem,) * 6,
        scratch_shapes=[
            pltpu.VMEM((4, PIECE, ROWS), bf16),
            pltpu.VMEM((3, ROWS, PIECE), bf16),
            pltpu.VMEM((PIECES, ROWS, PIECE), bf16),
            pltpu.VMEM((PIECES, PIECE, COLS), bf16),
            pltpu.VMEM((ROWS, 128), f32),
            pltpu.VMEM((8, ROWS // 128, 128), f32),
            pltpu.VMEM((16, 1, COLS), f32),
            pltpu.VMEM((32, 1, 128), f32),
            pltpu.VMEM((4, 1, 128), f32),
            pltpu.SemaphoreType.DMA((7,)),
            pltpu.SemaphoreType.DMA((SENDS,)),
            pltpu.SemaphoreType.DMA((PIECES + 2,)),
            pltpu.SemaphoreType.DMA((PIECES + 3,)),
            pltpu.SemaphoreType.DMA((16,)),
            pltpu.SemaphoreType.DMA((8,)),
            pltpu.SemaphoreType.DMA((32,)),
            pltpu.SemaphoreType.DMA((4,)),
            pltpu.SemaphoreType.DMA((8,)),
            pltpu.SemaphoreType.DMA((16,)),
            pltpu.SemaphoreType.DMA((32,)),
            pltpu.SemaphoreType.DMA((4,)),
        ],
        compiler_params=pltpu.CompilerParams(
            collective_id=0, has_side_effects=True, vmem_limit_bytes=38 << 20
        ),
    )(activations, cotangent, weight, row_moment.reshape(ROWS // 128, 128), col_moment.reshape(1, COLS))
    return pl.pallas_call(
        write_kernel,
        out_shape=(
            jax.ShapeDtypeStruct((ROWS, COLS), f32),
            jax.ShapeDtypeStruct((ROWS, COLS), bf16),
            jax.ShapeDtypeStruct((ROWS,), f32),
            jax.ShapeDtypeStruct((COLS,), f32),
        ),
        in_specs=[vmem] * 6,
        out_specs=(anywhere, anywhere, vmem, vmem),
        scratch_shapes=[
            pltpu.VMEM((6, 64, COLS), f32),
            pltpu.VMEM((6, 64, COLS), bf16),
            pltpu.SemaphoreType.DMA((6, 2)),
        ],
        compiler_params=pltpu.CompilerParams(vmem_limit_bytes=16 << 20),
    )(*held)


def solution(mesh):
    placed = (
        P(("dp", "col"), "row"),
        P(("dp", "row"), "col"),
        P(("row", "dp"), "col"),
        P(("row", "dp")),
        P("col"),
    )
    return jax.shard_map(
        body,
        mesh=mesh,
        in_specs=placed,
        out_specs=(P(("row", "dp"), "col"), P(("row", "dp"), "col"), P(("row", "dp")), P("col")),
        check_vma=False,
    )
```

```python
import functools

import jax
import jax.numpy as jnp
from jax import lax
from jax.experimental import pallas as pl
from jax.experimental.pallas import tpu as pltpu
from jax.sharding import PartitionSpec as P

D = 18432
F = 16384
STEP = 10
MESH = pl.DeviceIdType.MESH

ROWS = 1152
COLS = 2048
PIECE = 128
PIECES = 32
SENDS = 66


PARTS = {
    "a0": (0, ROWS // 2), "a1": (ROWS // 2, ROWS // 2),
    "c0": (0, 32), "c1": (32, 32), "c2": (64, 64),
}
PART_SEM = {"a0": 0, "a1": 1, "c0": 0, "c1": 1, "c2": 2}
ORDER = (
    ("a>", (0, 0, 0), "z+"), ("a>", (0, 0, 0), "z-"), ("c>", (0, 0, 0, 0), "core"), ("c>", (0, 0, 0, 1), "core"),
    ("c>", (0, 0, 0, 0), "z+"), ("c>", (0, 0, 0, 1), "z-"), ("c>", (0, 0, 0, 1), "x"), ("c<", (0, 0, 1, 0)),
    ("c<", (0, 0, 1, 1)), ("a<", (0, 0, -1)), ("a0>", (0, 0, -1), "y+"), ("a<", (0, 0, 1)), ("a1>", (0, 0, 1), "y-"),
    ("a<", (-1, 0, 0)), ("a>", (-1, 0, 0), "y+"), ("a>", (-1, 0, 0), "y-"), ("a<", (1, 0, 0)), ("a<", (0, 1, 0)),
    ("a0<", (0, 0, 2)), ("a>", (0, 1, 0), "y+"), ("a1<", (0, 0, 2)), ("a>", (0, 1, 0), "y-"), ("a>", (0, 0, 0), "z2"),
    ("a>", (1, 0, 0), "xh"), ("a<", (-1, 0, -1)), ("a>", (1, 0, 0), "y+"), ("a<", (-1, 0, 1)),
    ("a>", (1, 0, 0), "y-"), ("c<", (-1, 0, 0, 0)), ("c>", (-1, 0, 0, 0), "core"), ("c>", (0, 0, 0, 1), "z+"),
    ("c>", (0, 0, 0, 0), "z-"), ("a>", (-1, 0, 0), "xh"), ("c<", (1, 0, 0, 1)), ("c>", (1, 0, 0, 1), "core"),
    ("c<", (0, 1, 0, 1)), ("c>", (0, 1, 0, 1), "core"), ("c<", (-1, 0, 1, 0)), ("c<", (1, 0, 1, 1)),
    ("c<", (0, 1, 1, 1)), ("a<", (0, 1, -1)), ("a>", (-1, 0, -1), "y+"), ("a<", (0, 1, 1)), ("a>", (0, 1, 1), "y-"),
    ("a<", (2, 0, 0)), ("a<", (1, 1, 0)), ("a>", (2, 0, 0), "xh"), ("c>", (-1, 0, 0, 0), "z+"),
    ("c>", (0, 1, 0, 1), "z-"), ("a<", (1, 0, -1)), ("a>", (1, 1, 0), "y+"), ("a<", (1, 0, 1)),
    ("a>", (1, 1, 0), "y-"), ("a<", (-1, 1, 0)), ("c>", (0, 0, 0, 0), "x"), ("c<", (-1, 0, 0, 1)),
    ("c>", (-1, 0, 0, 1), "core"), ("c<", (1, 0, 0, 0)), ("c>", (1, 0, 0, 0), "core"), ("a<", (-1, 0, 2)),
    ("a>", (-1, 1, 0), "y+"), ("a<", (0, 1, 2)), ("a>", (-1, 1, 0), "y-"), ("mm", "zero_near"), ("a<", (2, 1, 0)),
    ("c<", (-1, 0, 1, 1)), ("c<", (1, 0, 1, 0)), ("c>", (0, 1, 0, 1), "z+"), ("c>", (1, 0, 0, 1), "z-"),
    ("a>", (-1, 0, 2), "xh"), ("a<", (1, 1, -1)), ("a>", (1, 1, -1), "y+"), ("a<", (1, 1, 1)),
    ("a>", (1, 0, 1), "y-"), ("mm", "plus_near"), ("c<", (2, 0, 0, 0)), ("c>", (2, 0, 0, 0), "core"),
    ("c<", (1, 1, 0, 1)), ("c>", (1, 1, 0, 1), "core"), ("c<", (0, 1, 0, 0)), ("c>", (0, 1, 0, 0), "core"),
    ("c>", (2, 0, 0, 0), "x"), ("a<", (-1, 1, -1)), ("a>", (2, 0, 0), "y+"), ("c<", (2, 0, 1, 0)),
    ("a>", (2, 1, 0), "y-"), ("a<", (-1, 1, 1)), ("mm", "minus_near"), ("c<", (1, 1, 1, 1)), ("c<", (0, 1, 1, 0)),
    ("mm", "zero_far"), ("c>", (0, 1, 0, 0), "z+"), ("c>", (0, 1, 0, 0), "z-"), ("a<", (-1, 1, 2)), ("a<", (1, 1, 2)),
    ("a>", (2, 1, 0), "y+"), ("a<", (1, 0, 2)), ("a>", (2, 0, 0), "y-"), ("mm", "near_last"), ("c<", (-1, 1, 0, 1)),
    ("c>", (-1, 1, 0, 1), "core"), ("c<", (2, 0, 0, 1)), ("c>", (2, 0, 0, 1), "core"), ("mm", "far_1_0"),
    ("c2>", (2, 0, 0, 1), "x"), ("c<", (-1, 1, 1, 1)), ("mm", "far_1_1"), ("c<", (2, 0, 1, 1)), ("a<", (2, 0, -1)),
    ("a>", (2, 0, -1), "y+"), ("a<", (2, 1, 1)), ("a>", (2, 1, 1), "y-"), ("c0>", (-1, 1, 0, 1), "z+"),
    ("c1>", (1, 1, 0, 1), "z-"), ("c<", (2, 1, 0, 0)), ("c>", (2, 1, 0, 0), "core"), ("a<", (2, 1, -1)),
    ("a<", (2, 0, 1)), ("mm", "two_near"), ("c<", (2, 1, 1, 0)), ("c<", (-1, 1, 0, 0)), ("c>", (-1, 1, 0, 0), "core"),
    ("c<", (1, 1, 0, 0)), ("c>", (1, 1, 0, 0), "core"), ("mm", "far_0_0"), ("c2<", (2, 1, 0, 1)),
    ("c0<", (2, 1, 0, 1)), ("c1<", (2, 1, 0, 1)), ("c>", (2, 1, 0, 1), "core"), ("mm", "two_side"),
    ("c<", (-1, 1, 1, 0)), ("c<", (1, 1, 1, 0)), ("mm", "far_0_1"), ("a<", (2, 0, 2)), ("a<", (2, 1, 2)),
    ("c<", (2, 1, 1, 1)), ("mm", "two_last"),
)


def gather_kernel(
    act, cot, weight, row_m, col_m,
    g_ref, w_ref, row_col, col_scale, row_out, col_out,
    a_in, a_src, at, ct, row_part, row_x, col_x, tot_a, tot_b,
    load_sem, send_sem, a_sem, c_sem, x_send, y_send, ta_send, tb_send, row_sem, col_sem, ta_sem, tb_sem,
):
    z, row, col = lax.axis_index("dp"), lax.axis_index("row"), lax.axis_index("col")
    x_lo, core = row // 2, row % 2
    x_hi, y = col // 4, col % 4
    group = z * 4 + row
    z_at = {o: lax.rem(z + o + 4, 4) for o in (0, 1, -1, 2)}
    y_at = {o: lax.rem(y + o + 4, 4) for o in (0, 1, -1, 2)}
    x_hi_at, x_lo_at, core_at = (x_hi, 1 - x_hi), (x_lo, 1 - x_lo), (core, 1 - core)

    def a_id(zo, xo, yo):
        return z_at[zo] * 8 + x_hi_at[xo] * 4 + y_at[yo]

    half_at = (lax.rem(y + 1, 2), lax.rem(y, 2))

    def c_id(zo, xo, co, half):
        return z_at[zo] * 8 + x_lo_at[xo] * 4 + core_at[co] * 2 + half_at[half]

    place = {
        "z+": {"dp": z_at[1], "row": row, "col": col},
        "z-": {"dp": z_at[-1], "row": row, "col": col},
        "z2": {"dp": z_at[2], "row": row, "col": col},
        "y+": {"dp": z, "row": row, "col": x_hi * 4 + y_at[1]},
        "y-": {"dp": z, "row": row, "col": x_hi * 4 + y_at[-1]},
        "xh": {"dp": z, "row": row, "col": (1 - x_hi) * 4 + y},
        "x": {"dp": z, "row": (1 - x_lo) * 2 + core, "col": col},
        "core": {"dp": z, "row": x_lo * 2 + 1 - core, "col": col},
    }

    def col_peer(i):
        return {"dp": z, "row": row, "col": lax.rem(col + i, 8)}

    def group_peer(i):
        return {"dp": lax.rem(z + i // 4, 4), "row": lax.rem(row + i, 4), "col": col}

    def group_slot(i):
        return lax.rem(z + i // 4, 4) * 4 + lax.rem(row + i, 4)

    def col_slot(i):
        return lax.rem(col + i, 8)

    def plane_peer(i):
        return {
            "dp": lax.rem(z + i // 8, 4), "row": lax.rem(row + i // 2 % 4, 4), "col": lax.rem(x_hi + i % 2, 2) * 4 + y,
        }

    def plane_slot(i):
        return (lax.rem(z + i // 8, 4) * 4 + lax.rem(row + i // 2 % 4, 4)) * 2 + lax.rem(x_hi + i % 2, 2)

    def y_peer(i):
        return {"dp": z, "row": row, "col": x_hi * 4 + lax.rem(y + i, 4)}

    def y_slot(i):
        return lax.rem(y + i, 4)

    barrier = pltpu.get_barrier_semaphore()
    for where in place.values():
        pl.semaphore_signal(barrier, inc=1, device_id=where, device_id_type=MESH)

    offsets = (0, 1, -1, 2)
    load_act = []
    for i, o in enumerate(offsets):
        start = pl.multiple_of(z_at[o] * ROWS, 128)
        load_act.append(pltpu.make_async_copy(act.at[:, pl.ds(start, ROWS)], a_in.at[i], load_sem.at[i]))
        load_act[i].start()
    mine_at = z * 8 + x_lo * 4 + core * 2
    load_cot = []
    for half in range(2):
        load_cot.append(pltpu.make_async_copy(
            cot.at[pl.ds(half * PIECE, PIECE)], ct.at[mine_at + half], load_sem.at[4 + half]
        ))
        load_cot[half].start()

    sent = []

    def push(src, dst, sem, device):
        copy = pltpu.make_async_remote_copy(
            src_ref=src, dst_ref=dst, send_sem=send_sem.at[len(sent)], recv_sem=sem,
            device_id=device, device_id_type=MESH,
        )
        copy.start()
        sent.append(copy)

    def piece(kind, key):
        if kind[0] == "a":
            t, whole, sem = a_id(*key), at, a_sem
        else:
            t, whole, sem = c_id(*key), ct, c_sem
        if kind in PARTS:
            return whole.at[t, pl.ds(*PARTS[kind])], sem.at[PIECES + PART_SEM[kind]]
        return whole.at[t], sem.at[t]

    def send(kind, key, where):
        ref, sem = piece(kind, key)
        push(ref, ref, sem, place[where])

    own = a_id(0, 0, 0)

    def turn(i, out):
        load_act[i].wait()
        for block in range(ROWS // 128):
            r = pl.ds(block * 128, 128)
            out[r, :] = a_in[i, :, r].T

    turn(0, at.at[own])
    pl.semaphore_wait(barrier, 8)
    for where in ("y+", "y-", "xh"):
        send("a", (0, 0, 0), where)
    for half in range(2):
        load_cot[half].wait()
    load_weight = pltpu.make_async_copy(weight, w_ref, load_sem.at[6])

    def matmul(ids, first=False, last=False, width=1024):
        def tile(j, carry):
            s = pl.ds(pl.multiple_of(j * width, width), width)
            left = jnp.concatenate([at[t] for t in ids], axis=1)
            right = jnp.concatenate([ct[t, :, s] for t in ids], axis=0)
            product = jnp.dot(left, right, preferred_element_type=jnp.float32)
            if not first:
                product = g_ref[:, s] + product
            g_ref[:, s] = product
            if last:
                square = product * product
                col_x[group, :, s] = jnp.sum(square, axis=0, keepdims=True)
                part = square[:, :128]
                for k in range(1, width // 128):
                    part = part + square[:, k * 128:(k + 1) * 128]
                row_part[...] += part
            return carry

        lax.fori_loop(0, COLS // width, tile, 0)

    def cot_group(zo, xo):
        return [c_id(zo, xo, co, half) for co in range(2) for half in range(2)]

    def far(half, *planes):
        return [c_id(zo, 1, co, half) for zo in (-1, 1) for co in planes]

    def meet(zo, xo, *steps):
        return [z_at[zo] * 8 + x_lo_at[xo] * 4 + y_at[yo] for yo in steps]

    groups = {
        "zero_near": cot_group(0, 0),
        "zero_far": cot_group(0, 1),
        "plus_near": meet(1, 0, 0, 1, -1),
        "minus_near": meet(-1, 0, 0, 1, -1),
        "near_last": meet(1, 0, 2) + meet(-1, 0, 2),
        "far_0": far(0, 0, 1),
        "far_1": far(1, 0, 1),
        "far_0_0": far(0, 0),
        "far_0_1": far(0, 1),
        "far_1_0": far(1, 0),
        "far_1_1": far(1, 1),
        "two_near": meet(2, 0, 0, 1, -1),
        "two_side": meet(2, 1, 1, -1),
        "two_last": meet(2, 1, 0, 2) + meet(2, 0, 2),
    }
    rounds = len([step for step in ORDER if step[0] == "mm"])

    multiplied = 0
    for step in ORDER:
        if step[0] == "mm":
            if multiplied == 0:
                load_weight.start()
                row_part[...] = jnp.zeros_like(row_part)
            multiplied += 1
            final = multiplied == rounds
            matmul(groups[step[1]], first=multiplied == 1, last=final, width=1024)
        elif step[0][-1] == ">":
            if step[0] == "a>" and step[1] == (0, 0, 0):
                i = ("z+", "z-", "z2").index(step[2])
                turn(i + 1, a_src.at[i])
                push(a_src.at[i], at.at[own], a_sem.at[own], place[step[2]])
            else:
                send(step[0][:-1], step[1], step[2])
        else:
            ref, sem = piece(step[0][:-1], step[1])
            pltpu.make_async_copy(ref, ref, sem).wait()

    def spread(buf, slot, sem, sends, peer, slots, count):
        copies = []
        for i in sorted(range(1, count), key=lambda i: abs(i // (count // 4) - 2)):
            copies.append(pltpu.make_async_remote_copy(
                src_ref=buf.at[slot], dst_ref=buf.at[slot], send_sem=sends.at[i], recv_sem=sem.at[slot],
                device_id=peer(i), device_id_type=MESH,
            ))
            copies[-1].start()

        def collect():
            for i in range(1, count):
                other = slots(i)
                pltpu.make_async_copy(buf.at[other], buf.at[other], sem.at[other]).wait()
            total = buf[0]
            for i in range(1, count):
                total = total + buf[i]
            return total

        sent.extend(copies)
        return collect

    col_collect = spread(col_x, group, col_sem, x_send, group_peer, group_slot, 16)
    for block in range(ROWS // 128):
        turned_part = row_part[pl.ds(block * 128, 128), :].T
        row_x[col, pl.ds(block, 1), :] = jnp.sum(turned_part, axis=0, keepdims=True)
    row_collect = spread(row_x, col, row_sem, y_send, col_peer, col_slot, 8)

    decay_rate = 1.0 - float(STEP) ** (-0.8)
    col_new = decay_rate * col_m[...] + (1.0 - decay_rate) * col_collect() / D
    col_out[...] = col_new
    col_scale[...] = lax.rsqrt(col_new)
    row_new = decay_rate * row_m[...] + (1.0 - decay_rate) * row_collect() / F
    row_out[...] = row_new
    row_scale = lax.rsqrt(row_new)
    for block in range(ROWS // 128):
        across = jnp.broadcast_to(row_scale[block:block + 1, :], (128, 128))
        row_col[pl.ds(block * 128, 128), :] = across.T

    def square_rows(block, total):
        r = pl.ds(pl.multiple_of(block * 128, 128), 128)
        line = jnp.zeros((128, 128), jnp.float32)
        for k in range(COLS // 128):
            s = pl.ds(k * 128, 128)
            value = g_ref[r, s] * col_scale[:, s]
            line = line + value * value
        factor = row_col[r, :]
        return total + line * factor * factor

    total = lax.fori_loop(0, ROWS // 128, square_rows, jnp.zeros((128, 128), jnp.float32))
    plane = group * 2 + x_hi
    tot_a[plane] = jnp.sum(total, axis=0, keepdims=True)
    a_collect = spread(tot_a, plane, ta_sem, ta_send, plane_peer, plane_slot, 32)
    tot_b[y] = a_collect()
    b_collect = spread(tot_b, y, tb_sem, tb_send, y_peer, y_slot, 4)
    for copy in sent:
        copy.wait_send()
    load_weight.wait()
    mean = jnp.sum(b_collect(), keepdims=True) / (D * F)
    clip_factor = jnp.maximum(1.0, jnp.sqrt(mean))
    col_scale[...] = col_scale[...] / clip_factor


def write_kernel(
    g_ref, w_ref, row_col, col_scale, row_new, col_new,
    new_weight, clipped, row_out, col_out, stage_w, stage_c, sem,
):
    relative = min(0.01, float(STEP) ** (-0.5))
    height, slots = 64, 6
    steps = ROWS // height

    def copies(i):
        r = pl.ds(i * height, height)
        s = i % slots
        return (
            pltpu.make_async_copy(stage_w.at[s], new_weight.at[r], sem.at[s, 0]),
            pltpu.make_async_copy(stage_c.at[s], clipped.at[r], sem.at[s, 1]),
        )

    for i in range(steps):
        if i >= slots:
            for copy in copies(i - slots):
                copy.wait()
        r = pl.ds(i * height, height)
        factor = row_col[r, :]
        for k in range(COLS // 128):
            s = pl.ds(k * 128, 128)
            value = g_ref[r, s] * factor * col_scale[:, s]
            stage_c[i % slots, :, s] = value.astype(jnp.bfloat16)
            stage_w[i % slots, :, s] = w_ref[r, s] - relative * value
        for copy in copies(i):
            copy.start()
    for block in range(ROWS // 128):
        row_out[pl.ds(block * 128, 128)] = row_new[block, :]
    for block in range(COLS // 128):
        col_out[pl.ds(block * 128, 128)] = col_new[0, block * 128:(block + 1) * 128]
    for i in range(steps - slots, steps):
        for copy in copies(i):
            copy.wait()


def body(activations, cotangent, weight, row_moment, col_moment):
    f32, bf16 = jnp.float32, jnp.bfloat16
    vmem, anywhere = pl.BlockSpec(memory_space=pltpu.VMEM), pl.BlockSpec(memory_space=pl.ANY)
    held = pl.pallas_call(
        gather_kernel,
        out_shape=(
            pltpu.VMEM((ROWS, COLS), f32),
            pltpu.VMEM((ROWS, COLS), f32),
            pltpu.VMEM((ROWS, 128), f32),
            pltpu.VMEM((1, COLS), f32),
            pltpu.VMEM((ROWS // 128, 128), f32),
            pltpu.VMEM((1, COLS), f32),
        ),
        in_specs=[anywhere, anywhere, anywhere, vmem, vmem],
        out_specs=(vmem,) * 6,
        scratch_shapes=[
            pltpu.VMEM((4, PIECE, ROWS), bf16),
            pltpu.VMEM((3, ROWS, PIECE), bf16),
            pltpu.VMEM((PIECES, ROWS, PIECE), bf16),
            pltpu.VMEM((PIECES, PIECE, COLS), bf16),
            pltpu.VMEM((ROWS, 128), f32),
            pltpu.VMEM((8, ROWS // 128, 128), f32),
            pltpu.VMEM((16, 1, COLS), f32),
            pltpu.VMEM((32, 1, 128), f32),
            pltpu.VMEM((4, 1, 128), f32),
            pltpu.SemaphoreType.DMA((7,)),
            pltpu.SemaphoreType.DMA((SENDS,)),
            pltpu.SemaphoreType.DMA((PIECES + 2,)),
            pltpu.SemaphoreType.DMA((PIECES + 3,)),
            pltpu.SemaphoreType.DMA((16,)),
            pltpu.SemaphoreType.DMA((8,)),
            pltpu.SemaphoreType.DMA((32,)),
            pltpu.SemaphoreType.DMA((4,)),
            pltpu.SemaphoreType.DMA((8,)),
            pltpu.SemaphoreType.DMA((16,)),
            pltpu.SemaphoreType.DMA((32,)),
            pltpu.SemaphoreType.DMA((4,)),
        ],
        compiler_params=pltpu.CompilerParams(
            collective_id=0, has_side_effects=True, vmem_limit_bytes=38 << 20
        ),
    )(activations, cotangent, weight, row_moment.reshape(ROWS // 128, 128), col_moment.reshape(1, COLS))
    return pl.pallas_call(
        write_kernel,
        out_shape=(
            jax.ShapeDtypeStruct((ROWS, COLS), f32),
            jax.ShapeDtypeStruct((ROWS, COLS), bf16),
            jax.ShapeDtypeStruct((ROWS,), f32),
            jax.ShapeDtypeStruct((COLS,), f32),
        ),
        in_specs=[vmem] * 6,
        out_specs=(anywhere, anywhere, vmem, vmem),
        scratch_shapes=[
            pltpu.VMEM((6, 64, COLS), f32),
            pltpu.VMEM((6, 64, COLS), bf16),
            pltpu.SemaphoreType.DMA((6, 2)),
        ],
        compiler_params=pltpu.CompilerParams(vmem_limit_bytes=16 << 20),
    )(*held)


def solution(mesh):
    placed = (
        P(("dp", "col"), "row"),
        P(("dp", "row"), "col"),
        P(("row", "dp"), "col"),
        P(("row", "dp")),
        P("col"),
    )
    return jax.shard_map(
        body,
        mesh=mesh,
        in_specs=placed,
        out_specs=(P(("row", "dp"), "col"), P(("row", "dp"), "col"), P(("row", "dp")), P("col")),
        check_vma=False,
    )
```
